32 devices in a mesh: gy: 8 (over z, core), gx: 4 (over y, x).
Axes of the slice: x: 2, y: 2, z: 4, core: 2. Of those that a mesh axis runs over, the one named last changes fastest.
Arguments:
- images: bfloat16 [16, 448, 1344], P(None, 'gy', 'gx'), may hold values from -6 to 6
- position: bfloat16 [32, 32, 768], P('gy', 'gx'), may hold values from -4 to 4
- stem_w: bfloat16 [27, 32], replicated, may hold values from -1.25 to 1.25
- stem_b: float32 [32], replicated, may hold values from -0.5 to 0.5
- patch_w: bfloat16 [6272, 768], replicated, may hold values from -0.078125 to 0.078125
- norm_one: float32 [768], replicated, may hold values from 0.25 to 1.75
- qkv_w: bfloat16 [768, 2304], replicated, may hold values from -0.21875 to 0.21875
- q_gain: float32 [768], replicated, may hold values from 0.8 to 5, as said below
- k_gain: float32 [768], replicated, may hold values from 0.8 to 5, as said below
- out_w: bfloat16 [768, 768], replicated, may hold values from -0.21875 to 0.21875
- norm_two: float32 [768], replicated, may hold values from 0.25 to 1.75
- mlp_in: bfloat16 [768, 3072], replicated, may hold values from -0.21875 to 0.21875
- mlp_out: bfloat16 [3072, 768], replicated, may hold values from -0.109375 to 0.109375
- norm_last: float32 [768], replicated, may hold values from 0.25 to 1.75
- head_w: bfloat16 [768, 1024], replicated, may hold values from -0.21875 to 0.21875
- head_b: float32 [1024], replicated, may hold values from -5 to 5
- dataset_action: int32 [16], replicated, may hold values from 0 to 1023
- sampled: int32 [16, 10], replicated, may hold values from 0 to 1023
- targets: float32 [16], replicated, may hold values from -5 to 5
Outputs:
- q_values: float32 [16, 1024], replicated
- frame_loss: float32 [16], replicated
- loss: float32 [], replicated
The draws below stay inside these ranges and needn't reach their ends.
Inputs may be any that keep to these rules, and one draw needn't show every extreme that they name: `q_gain`: gains of the query and key norms are positive. `k_gain`: gains of the query and key norms are positive. `sampled`: sampled actions of a frame may repeat.
All inputs are finite; a program needn't handle non-finite values.
Results may differ from the reference program's by a relative error of at most 0.00073.
Values may be sent and summed in bfloat16 or wider, within the bound.
A program may use at most 192 MiB of HBM per device.

```python
import jax
import jax.numpy as jnp
from jax import lax

D = 768
HEADS = 12
HEAD_DIM = 64
FF = 3072
STEM = 32
PATCH = 14
ACTIONS = 1024
SAMPLES = 10
FRAMES = 16
GRID_R = 32
GRID_C = 32
TOKENS = 1024
HEIGHT = 448
WIDTH = 448


def draw_q_gain(key, part):
    return jax.random.uniform(jax.random.fold_in(key, 11), (D,), jnp.float32, 0.8, 2.0)


def draw_k_gain(key, part):
    return jax.random.uniform(jax.random.fold_in(key, 23), (D,), jnp.float32, 0.8, 2.0)


def place_ends(values, own_key, low, high):
    spot = [jax.random.randint(jax.random.fold_in(own_key, axis), (), 0, length) for axis, length in enumerate(values.shape)]
    main_axis = values.shape.index(max(values.shape))
    neighbour = spot[:main_axis] + [(spot[main_axis] + 1) % values.shape[main_axis]] + spot[main_axis + 1:]
    return values.at[tuple(spot)].set(low).at[tuple(neighbour)].set(high)


def levels(own_key, dims, pieces, smallest, high):
    def one(dim, blocks):
        draws = jax.random.uniform(jax.random.fold_in(jax.random.fold_in(own_key, 6), dim), (blocks,), jnp.float32, smallest / len(pieces), high / len(pieces))
        return jnp.repeat(jnp.exp(draws), dims[dim] // blocks).reshape((-1,) + (1,) * (len(dims) - dim - 1))

    loudness = one(*pieces[0])
    for cut in pieces[1:]:
        loudness = loudness * one(*cut)
    return loudness


def centred(own_key, shape, scale, bound, pieces=(), kind=jnp.bfloat16):
    values = scale * jax.random.normal(own_key, shape, jnp.float32)
    if pieces:
        values = values * levels(own_key, shape, pieces, -0.22, 0.18)
    return jnp.clip(values, -bound, bound).astype(kind)


def setup_inputs(seed: int = 0) -> dict:
    streams_of = jax.random.split(jax.random.key(seed), 20)
    images = centred(streams_of[0], (FRAMES, HEIGHT, WIDTH * 3), 1.0, 6.0, ((1, 8), (2, 4)))
    position = centred(streams_of[1], (GRID_R, GRID_C, D), 0.5, 4.0, ((0, 8), (1, 4)))
    stem_w = centred(streams_of[2], (27, STEM), 27 ** -0.5, 1.25)
    stem_b = jnp.clip(jax.random.uniform(streams_of[3], (STEM,), jnp.float32, -0.5, 0.5), -0.5, 0.5)
    patch_w = centred(streams_of[4], (PATCH * PATCH * STEM, D), (PATCH * PATCH * STEM) ** -0.5, 0.078125)
    norm_one = jnp.clip(1.0 + 0.15 * jax.random.normal(streams_of[5], (D,), jnp.float32), 0.25, 1.75)
    qkv_w = centred(streams_of[6], (D, 3 * D), D ** -0.5, 0.21875)
    q_gain = draw_q_gain(jax.random.fold_in(streams_of[19], 71), 0)
    k_gain = draw_k_gain(jax.random.fold_in(streams_of[19], 71), 0)
    out_w = centred(streams_of[9], (D, D), D ** -0.5, 0.21875)
    norm_two = jnp.clip(1.0 + 0.15 * jax.random.normal(streams_of[10], (D,), jnp.float32), 0.25, 1.75)
    mlp_in = centred(streams_of[11], (D, FF), D ** -0.5, 0.21875)
    mlp_out = centred(streams_of[12], (FF, D), FF ** -0.5, 0.109375)
    norm_last = jnp.clip(1.0 + 0.15 * jax.random.normal(streams_of[13], (D,), jnp.float32), 0.25, 1.75)
    head_w = centred(streams_of[14], (D, ACTIONS), D ** -0.5, 0.21875)
    head_b = centred(streams_of[15], (ACTIONS,), 1.0, 5.0, (), jnp.float32)
    dataset_action = place_ends(jax.random.randint(streams_of[16], (FRAMES,), 0, ACTIONS), jax.random.fold_in(streams_of[16], 1), 0, ACTIONS - 1).astype(jnp.int32)
    sampled = place_ends(jax.random.randint(streams_of[17], (FRAMES, SAMPLES), 0, ACTIONS), jax.random.fold_in(streams_of[17], 1), 0, ACTIONS - 1).astype(jnp.int32)
    targets = centred(streams_of[18], (FRAMES,), 1.0, 5.0, (), jnp.float32)
    return dict(images=images, position=position, stem_w=stem_w, stem_b=stem_b, patch_w=patch_w, norm_one=norm_one, qkv_w=qkv_w, q_gain=q_gain, k_gain=k_gain, out_w=out_w, norm_two=norm_two, mlp_in=mlp_in, mlp_out=mlp_out, norm_last=norm_last, head_w=head_w, head_b=head_b, dataset_action=dataset_action, sampled=sampled, targets=targets)


eps = 1e-06
penalty_weight = 1.0

def layer_norm(values, gain):
    centre = values - lax.optimization_barrier(jnp.mean(values, -1, keepdims=True))
    spread = lax.optimization_barrier(jnp.mean(centre * centre, -1, keepdims=True))
    return centre * lax.rsqrt(spread + eps) * gain

def head_scale(values, gain):
    shaped = values.reshape(values.shape[:-1] + (HEADS, HEAD_DIM))
    shaped = shaped * lax.rsqrt(lax.optimization_barrier(jnp.mean(shaped * shaped, -1, keepdims=True)) + eps)
    return shaped.reshape(values.shape) * gain

def reference(images, position, stem_w, stem_b, patch_w, norm_one, qkv_w, q_gain, k_gain, out_w, norm_two, mlp_in, mlp_out, norm_last, head_w, head_b, dataset_action, sampled, targets):
    query_len = 512 if TOKENS % 512 == 0 else TOKENS
    place = position.reshape(TOKENS, D).astype(jnp.float32)

    def frame_pooled(image):
        pixels = image.reshape(HEIGHT, WIDTH, 3)
        padded = jnp.pad(pixels, ((1, 1), (1, 1), (0, 0)))
        taps = jnp.concatenate([padded[row_off:row_off + HEIGHT, col_off:col_off + WIDTH, :] for row_off in range(3) for col_off in range(3)], -1)
        conv = jnp.einsum('hwt,tc->hwc', taps.astype(jnp.float32), stem_w.astype(jnp.float32))
        stem = jax.nn.gelu(conv + stem_b).astype(jnp.bfloat16)
        patches = stem.reshape(GRID_R, PATCH, GRID_C, PATCH, STEM).transpose(0, 2, 1, 3, 4).reshape(TOKENS, PATCH * PATCH * STEM)
        embedded = (jnp.dot(patches, patch_w, preferred_element_type=jnp.float32) + place).astype(jnp.bfloat16)
        normed = layer_norm(embedded.astype(jnp.float32), norm_one).astype(jnp.bfloat16)
        packed = jnp.dot(normed, qkv_w, preferred_element_type=jnp.float32)
        queries = (head_scale(packed[:, :D], q_gain) * HEAD_DIM ** (-0.5)).astype(jnp.bfloat16)
        keys = head_scale(packed[:, D:2 * D], k_gain).astype(jnp.bfloat16)
        values = packed[:, 2 * D:].astype(jnp.bfloat16)
        keys_f = keys.reshape(TOKENS, HEADS, HEAD_DIM).astype(jnp.float32)
        values_f = values.reshape(TOKENS, HEADS, HEAD_DIM).astype(jnp.float32)

        def attend(block):
            scores = jnp.einsum('qhd,khd->hqk', block.astype(jnp.float32), keys_f)
            top = lax.optimization_barrier(jnp.max(scores, -1, keepdims=True))
            expd = jnp.exp(scores - top)
            totals = lax.optimization_barrier(jnp.sum(expd, -1))
            weights = expd.astype(jnp.bfloat16).astype(jnp.float32)
            result = jnp.einsum('hqk,khd->qhd', weights, values_f) / jnp.transpose(totals)[:, :, None]
            return result.reshape(query_len, D).astype(jnp.bfloat16)
        attended = lax.map(attend, queries.reshape(TOKENS // query_len, query_len, HEADS, HEAD_DIM)).reshape(TOKENS, D)
        stream = embedded.astype(jnp.float32) + jnp.dot(attended, out_w, preferred_element_type=jnp.float32)
        normed2 = layer_norm(stream, norm_two).astype(jnp.bfloat16)
        hidden = jax.nn.gelu(jnp.dot(normed2, mlp_in, preferred_element_type=jnp.float32)).astype(jnp.bfloat16)
        final = stream + jnp.dot(hidden, mlp_out, preferred_element_type=jnp.float32)
        return lax.optimization_barrier(jnp.mean(layer_norm(final, norm_last), 0))
    pooled = lax.map(frame_pooled, images)
    q_values = jnp.dot(pooled, head_w.astype(jnp.float32), precision=lax.Precision.HIGHEST) + head_b
    columns = jnp.arange(ACTIONS, dtype=jnp.int32)
    picked = lax.optimization_barrier(jnp.sum(jnp.where(sampled[:, :, None] == columns, q_values[:, None, :], 0.0), -1))
    chosen = lax.optimization_barrier(jnp.sum(jnp.where(dataset_action[:, None] == columns, q_values, 0.0), -1))
    top = lax.optimization_barrier(jnp.max(picked, -1))
    spread = top + jnp.log(lax.optimization_barrier(jnp.sum(jnp.exp(picked - top[:, None]), -1)))
    frame_loss = penalty_weight * (spread - chosen) + 0.5 * (chosen - targets) ** 2
    return (q_values, frame_loss, jnp.mean(frame_loss))
```

```python
import functools

import jax
import jax.numpy as jnp
import numpy as np
from jax import lax
from jax.experimental import pallas as pl
from jax.experimental.pallas import tpu as pltpu
from jax.sharding import PartitionSpec as P

HEAD_DIM = 64
PATCH = 14
eps = 1e-06
penalty_weight = 1.0
F32 = jnp.float32
BF16 = jnp.bfloat16
MESH = pl.DeviceIdType.MESH
VMEM_LIMIT = 56 * 1024 * 1024


def vmem():
    return pl.BlockSpec(memory_space=pltpu.VMEM)


def gelu(x):
    u = x * (0.7978845608028654 + (0.7978845608028654 * 0.044715) * (x * x))
    half = 0.5 * x
    return half + half * jnp.tanh(u)


def layer_norm(values, gain):
    centre = values - jnp.mean(values, -1, keepdims=True)
    spread = jnp.mean(centre * centre, -1, keepdims=True)
    return centre * lax.rsqrt(spread + eps) * gain


def borders(images):
    tall = jnp.transpose(images, (1, 0, 2))
    for axis, dim, width in (("gy", 0, 1), ("gx", 2, 3)):
        ends = lax.axis_size(axis) - 1
        head = lax.slice_in_dim(tall, 0, width, axis=dim)
        tail = lax.slice_in_dim(tall, tall.shape[dim] - width, tall.shape[dim], axis=dim)
        before = lax.ppermute(tail, axis, [(i, i + 1) for i in range(ends)])
        after = lax.ppermute(head, axis, [(i + 1, i) for i in range(ends)])
        tall = jnp.concatenate([before, tall, after], axis=dim)
    return tall


def band(stem_w):
    channels = stem_w.shape[1]
    rows = np.arange(9 * (PATCH + 2))
    row_off, rest = rows // (3 * (PATCH + 2)), rows % (3 * (PATCH + 2))
    col_in, colour = rest // 3, rest % 3
    col_out = np.arange(PATCH * channels) // channels
    wide = jnp.tile(stem_w, (1, PATCH))
    picks = np.zeros((3, rows.size, 27), np.float32)
    for col_off in range(3):
        picks[col_off, rows, row_off * 9 + col_off * 3 + colour] = 1
    spread = jnp.dot(jnp.asarray(picks.reshape(-1, 27), BF16), wide, preferred_element_type=F32)
    spread = spread.reshape(3, rows.size, -1)
    total = 0.0
    for col_off in range(3):
        keep = col_in[:, None] == col_out[None, :] + col_off
        total = total + jnp.where(keep, spread[col_off], 0.0)
    return total.astype(BF16)


def embed_kernel(tall_ref, pos_ref, band_ref, bias_ref, pw_hbm, out_ref, stem, pw, acc, sem):
    rows, frames, _ = tall_ref.shape
    rows = rows - 2
    patch_rows, patch_cols, width = pos_ref.shape
    feats = band_ref.shape[1]
    span = 3 * (PATCH + 2)
    load = pltpu.make_async_copy(pw_hbm, pw, sem)
    load.start()
    for col in range(patch_cols):
        cut = tall_ref[:, :, 3 * PATCH * col : 3 * PATCH * col + span]
        taps = jnp.concatenate([cut[off : off + rows] for off in range(3)], axis=-1)
        for i in range(patch_rows):
            part = taps[i * PATCH : (i + 1) * PATCH].reshape(PATCH * frames, 3 * span)
            conv = jnp.dot(part, band_ref[...], preferred_element_type=F32)
            made = gelu(conv + bias_ref[...]).astype(BF16)
            stem[:, col, i] = made.reshape(PATCH, frames, feats)
    load.wait()
    count = patch_cols * patch_rows * frames
    acc[...] = jnp.zeros_like(acc)

    def step(p, carry):
        acc[...] += jnp.dot(
            stem[p].reshape(count, feats),
            pw[pl.ds(pl.multiple_of(p * feats, 64), feats), :],
            preferred_element_type=F32,
        )
        return carry

    lax.fori_loop(0, PATCH, step, 0)
    pieces = []
    for col in range(patch_cols):
        for i in range(patch_rows):
            at = (col * patch_rows + i) * frames
            place = pos_ref[i, col : col + 1, :].astype(F32)
            pieces.append((acc[at : at + frames, :] + place).astype(BF16))
    made = jnp.concatenate(pieces, axis=0)
    tiles = patch_cols * patch_rows
    to = lax.broadcasted_iota(jnp.int32, (count, count), 0)
    fro = lax.broadcasted_iota(jnp.int32, (count, count), 1)
    swap = jnp.where((to % tiles) * frames + to // tiles == fro, 1.0, 0.0).astype(BF16)
    out_ref[...] = (
        jnp.dot(swap, made, preferred_element_type=F32).astype(BF16).reshape(frames, tiles, width)
    )


def embed(tall, position, stem_w, stem_b, patch_w):
    patch_rows, patch_cols, width = position.shape
    frames = tall.shape[1]
    feats = PATCH * stem_w.shape[1]
    count = patch_rows * patch_cols * frames
    return pl.pallas_call(
        embed_kernel,
        out_shape=jax.ShapeDtypeStruct((frames, patch_rows * patch_cols, width), BF16),
        in_specs=[vmem()] * 4 + [pl.BlockSpec(memory_space=pl.ANY)],
        out_specs=vmem(),
        scratch_shapes=[
            pltpu.VMEM((PATCH, patch_cols, patch_rows, frames, feats), BF16),
            pltpu.VMEM(patch_w.shape, BF16),
            pltpu.VMEM((count, width), F32),
            pltpu.SemaphoreType.DMA,
        ],
        compiler_params=pltpu.CompilerParams(vmem_limit_bytes=VMEM_LIMIT),
        name="embed",
    )(tall, position, band(stem_w), jnp.tile(stem_b, PATCH)[None, :], patch_w)


def regroup_kernel(n_gx, group, src_ref, out_ref, send_sem, recv_sem, own_sem):
    frames = src_ref.shape[0]
    gy, gx = lax.axis_index("gy"), lax.axis_index("gx")
    low = lax.rem(gy, group)
    me = (gy // group) * n_gx + gx

    def device(frame):
        return ((frame // n_gx) * group + low, lax.rem(frame, n_gx))

    barrier = pltpu.get_barrier_semaphore()

    def greet(k, carry):
        pl.semaphore_signal(
            barrier, inc=1, device_id=device(lax.rem(me + k, frames)), device_id_type=MESH
        )
        return carry

    lax.fori_loop(1, frames, greet, 0)
    own = pltpu.make_async_copy(src_ref.at[me], out_ref.at[me], own_sem)
    own.start()
    pl.semaphore_wait(barrier, frames - 1)

    def copy(k):
        to = lax.rem(me + k, frames)
        return pltpu.make_async_remote_copy(
            src_ref=src_ref.at[to],
            dst_ref=out_ref.at[me],
            send_sem=send_sem.at[k],
            recv_sem=recv_sem.at[k],
            device_id=device(to),
            device_id_type=MESH,
        )

    def start(k, carry):
        copy(k).start()
        return carry

    def finish(k, carry):
        fro = lax.rem(me - k + frames, frames)
        pltpu.make_async_remote_copy(
            src_ref=src_ref.at[fro],
            dst_ref=out_ref.at[fro],
            send_sem=send_sem.at[k],
            recv_sem=recv_sem.at[k],
            device_id=device(fro),
            device_id_type=MESH,
        ).wait()
        return carry

    lax.fori_loop(1, frames, start, 0)
    lax.fori_loop(1, frames, finish, 0)
    own.wait()


def regroup(embedded, n_gx, group):
    frames = embedded.shape[0]
    return pl.pallas_call(
        functools.partial(regroup_kernel, n_gx, group),
        out_shape=jax.ShapeDtypeStruct(embedded.shape, BF16),
        in_specs=[vmem()],
        out_specs=vmem(),
        scratch_shapes=[
            pltpu.SemaphoreType.DMA((frames,)),
            pltpu.SemaphoreType.DMA((frames,)),
            pltpu.SemaphoreType.DMA,
        ],
        compiler_params=pltpu.CompilerParams(collective_id=0, has_side_effects=True),
        name="regroup",
    )(embedded)


def head_scale(tile, gain):
    left = lax.broadcasted_iota(jnp.int32, tile.shape, 1) < HEAD_DIM
    square = tile * tile
    one = jnp.sum(jnp.where(left, square, 0.0), -1, keepdims=True)
    two = jnp.sum(jnp.where(left, 0.0, square), -1, keepdims=True)
    scale = lax.rsqrt(jnp.where(left, one, two) * (1.0 / HEAD_DIM) + eps)
    return tile * scale * gain


def project_kernel(seq_ref, norm_ref, w_ref, qg_ref, kg_ref, q_ref, kv_ref):
    width = seq_ref.shape[1]
    normed = layer_norm(seq_ref[...].astype(F32), norm_ref[...]).astype(BF16)
    pair = 2 * HEAD_DIM
    for at in range(0, 3 * width, 2 * pair):
        both = jnp.dot(normed, w_ref[:, at : at + 2 * pair], preferred_element_type=F32)
        for half in range(2):
            tile = both[:, half * pair : (half + 1) * pair]
            here = at % width + half * pair
            lanes = slice(here, here + pair)
            if at < width:
                made = head_scale(tile, qg_ref[:, lanes]) * HEAD_DIM ** (-0.5)
                q_ref[:, lanes] = made.astype(BF16)
            elif at < 2 * width:
                kv_ref[0, :, lanes] = head_scale(tile, kg_ref[:, lanes]).astype(BF16)
            else:
                kv_ref[1, :, lanes] = tile.astype(BF16)


def project(seq, norm_one, qkv_w, q_gain, k_gain):
    count, width = seq.shape
    return pl.pallas_call(
        project_kernel,
        out_shape=(
            jax.ShapeDtypeStruct((count, width), BF16),
            jax.ShapeDtypeStruct((2, count, width), BF16),
        ),
        in_specs=[vmem()] * 5,
        out_specs=(vmem(), vmem()),
        compiler_params=pltpu.CompilerParams(vmem_limit_bytes=VMEM_LIMIT),
        name="project",
    )(seq, norm_one[None, :], qkv_w, q_gain[None, :], k_gain[None, :])


def share_kernel(group, src_ref, out_ref, send_sem, recv_sem, own_sem):
    gy, gx = lax.axis_index("gy"), lax.axis_index("gx")
    low = lax.rem(gy, group)
    base = gy - low

    def device(other):
        return (base + other, gx)

    barrier = pltpu.get_barrier_semaphore()

    def greet(k, carry):
        pl.semaphore_signal(
            barrier, inc=1, device_id=device(lax.rem(low + k, group)), device_id_type=MESH
        )
        return carry

    lax.fori_loop(1, group, greet, 0)
    own = pltpu.make_async_copy(src_ref, out_ref.at[low], own_sem)
    own.start()
    pl.semaphore_wait(barrier, group - 1)

    def copy(k, slot):
        return pltpu.make_async_remote_copy(
            src_ref=src_ref,
            dst_ref=out_ref.at[slot],
            send_sem=send_sem.at[k],
            recv_sem=recv_sem.at[k],
            device_id=device(lax.rem(low + k, group)),
            device_id_type=MESH,
        )

    def start(k, carry):
        copy(k, low).start()
        return carry

    def finish(k, carry):
        copy(k, lax.rem(low - k + group, group)).wait()
        return carry

    lax.fori_loop(1, group, start, 0)
    lax.fori_loop(1, group, finish, 0)
    own.wait()


def share(kv, group):
    if group == 1:
        return kv[None]
    return pl.pallas_call(
        functools.partial(share_kernel, group),
        out_shape=jax.ShapeDtypeStruct((group,) + kv.shape, BF16),
        in_specs=[vmem()],
        out_specs=vmem(),
        scratch_shapes=[
            pltpu.SemaphoreType.DMA((group,)),
            pltpu.SemaphoreType.DMA((group,)),
            pltpu.SemaphoreType.DMA,
        ],
        compiler_params=pltpu.CompilerParams(
            collective_id=1, has_side_effects=True, vmem_limit_bytes=VMEM_LIMIT
        ),
        name="share",
    )(kv)


def layer_kernel(
    seq_ref, q_ref, kv_ref, ow_ref, norm2_ref, wi_hbm, wo_hbm, last_ref, out_ref,
    attended, wi, wo, sems,
):
    count, width = seq_ref.shape
    group = kv_ref.shape[0]
    hidden = wi.shape[1]
    loads = [
        pltpu.make_async_copy(wi_hbm, wi, sems.at[0]),
        pltpu.make_async_copy(wo_hbm, wo, sems.at[1]),
    ]
    for load in loads:
        load.start()
    pair = 2 * HEAD_DIM
    block = 256

    def attend(lanes, rows):
        q = q_ref[rows, lanes]
        left = lax.broadcasted_iota(jnp.int32, q.shape, 1) < HEAD_DIM
        halves = []
        for side in range(2):
            mine = jnp.where(left if side == 0 else jnp.logical_not(left), q, jnp.zeros_like(q))
            scores = [
                lax.dot_general(
                    mine, kv_ref[g, 0, :, lanes], (((1,), (1,)), ((), ())),
                    preferred_element_type=F32,
                )
                for g in range(group)
            ]
            top = functools.reduce(
                jnp.maximum, [jnp.max(part, -1, keepdims=True) for part in scores]
            )
            totals, made = 0.0, 0.0
            for g in range(group):
                expd = jnp.exp(scores[g] - top)
                totals = totals + jnp.sum(expd, -1, keepdims=True)
                made = made + jnp.dot(
                    expd.astype(BF16), kv_ref[g, 1, :, lanes], preferred_element_type=F32
                )
            halves.append(made / totals)
        attended[rows, lanes] = jnp.where(left, halves[0], halves[1]).astype(BF16)

    depth = max(32, 2 * block // group)

    def each(step, carry):
        at = pl.multiple_of((step // (count // depth)) * pair, pair)
        low = pl.multiple_of(lax.rem(step, count // depth) * depth, depth)
        attend(pl.ds(at, pair), pl.ds(low, depth))
        return carry

    lax.fori_loop(0, (width // pair) * (count // depth), each, 0)

    for load in loads:
        load.wait()
    total = jnp.zeros((1, width), F32)
    for low in range(0, count, block):
        rows = slice(low, low + block)
        stream = seq_ref[rows, :].astype(F32) + jnp.dot(
            attended[rows, :], ow_ref[...], preferred_element_type=F32
        )
        normed = layer_norm(stream, norm2_ref[...]).astype(BF16)
        final = stream
        for at in range(0, hidden, width):
            inner = gelu(
                jnp.dot(normed, wi[:, at : at + width], preferred_element_type=F32)
            ).astype(BF16)
            final = final + jnp.dot(inner, wo[at : at + width, :], preferred_element_type=F32)
        total = total + jnp.sum(layer_norm(final, last_ref[...]), 0, keepdims=True)
    out_ref[...] = total


def layer(seq, q, kv, out_w, norm_two, mlp_in, mlp_out, norm_last):
    count, width = seq.shape
    anywhere = pl.BlockSpec(memory_space=pl.ANY)
    return pl.pallas_call(
        layer_kernel,
        out_shape=jax.ShapeDtypeStruct((1, width), F32),
        in_specs=[vmem()] * 5 + [anywhere, anywhere, vmem()],
        out_specs=vmem(),
        scratch_shapes=[
            pltpu.VMEM((count, width), BF16),
            pltpu.VMEM(mlp_in.shape, BF16),
            pltpu.VMEM(mlp_out.shape, BF16),
            pltpu.SemaphoreType.DMA((2,)),
        ],
        compiler_params=pltpu.CompilerParams(vmem_limit_bytes=VMEM_LIMIT),
        name="layer",
    )(seq, q, kv, out_w, norm_two[None, :], mlp_in, mlp_out, norm_last[None, :])


def collect_kernel(n_gx, count, src_ref, out_ref, send_sem, recv_sem, own_sem):
    gy, gx = lax.axis_index("gy"), lax.axis_index("gx")
    me = gy * n_gx + gx

    def device(other):
        return (other // n_gx, lax.rem(other, n_gx))

    barrier = pltpu.get_barrier_semaphore()

    def greet(k, carry):
        pl.semaphore_signal(
            barrier, inc=1, device_id=device(lax.rem(me + k, count)), device_id_type=MESH
        )
        return carry

    lax.fori_loop(1, count, greet, 0)
    own = pltpu.make_async_copy(src_ref, out_ref.at[me], own_sem)
    own.start()
    pl.semaphore_wait(barrier, count - 1)

    def copy(k, slot):
        return pltpu.make_async_remote_copy(
            src_ref=src_ref,
            dst_ref=out_ref.at[slot],
            send_sem=send_sem.at[k],
            recv_sem=recv_sem.at[k],
            device_id=device(lax.rem(me + k, count)),
            device_id_type=MESH,
        )

    def start(k, carry):
        copy(k, me).start()
        return carry

    def finish(k, carry):
        copy(k, lax.rem(me - k + count, count)).wait()
        return carry

    lax.fori_loop(1, count, start, 0)
    lax.fori_loop(1, count, finish, 0)
    own.wait()


def collect(partial, n_gx, count):
    return pl.pallas_call(
        functools.partial(collect_kernel, n_gx, count),
        out_shape=jax.ShapeDtypeStruct((count,) + partial.shape, F32),
        in_specs=[vmem()],
        out_specs=vmem(),
        scratch_shapes=[
            pltpu.SemaphoreType.DMA((count,)),
            pltpu.SemaphoreType.DMA((count,)),
            pltpu.SemaphoreType.DMA,
        ],
        compiler_params=pltpu.CompilerParams(collective_id=2, has_side_effects=True),
        name="collect",
    )(partial)


def critic_kernel(
    sums_ref, w_ref, b_ref, act_ref, samp_ref, targ_ref, q_ref, loss_ref, mean_ref, *, n_gx, tokens
):
    count, _, width = sums_ref.shape
    frames, actions = q_ref.shape
    group = count // frames
    rows = []
    for frame in range(frames):
        high, gx = frame // n_gx, frame % n_gx
        part = 0.0
        for low in range(group):
            part = part + sums_ref[(high * group + low) * n_gx + gx]
        rows.append(part)
    pooled = jnp.concatenate(rows, axis=0) / tokens
    q = b_ref[...] + jnp.zeros((frames, actions), F32)
    rest = pooled
    made = 0.0
    for _ in range(3):
        piece = rest.astype(BF16)
        rest = rest - piece.astype(F32)
        made = made + jnp.dot(piece, w_ref[...], preferred_element_type=F32)
    q = made + b_ref[...]
    q_ref[...] = q
    columns = lax.broadcasted_iota(jnp.int32, (frames, actions), 1)

    def pick(index):
        return jnp.sum(jnp.where(index == columns, q, 0.0), -1, keepdims=True)

    chosen = pick(act_ref[...])
    picked = [pick(samp_ref[:, s : s + 1]) for s in range(samp_ref.shape[1])]
    top = functools.reduce(jnp.maximum, picked)
    total = sum(jnp.exp(one - top) for one in picked)
    spread = top + jnp.log(total)
    loss = penalty_weight * (spread - chosen) + 0.5 * (chosen - targ_ref[...]) ** 2
    loss_ref[...] = loss
    mean_ref[...] = jnp.mean(loss, 0, keepdims=True)


def critic(sums, head_w, head_b, dataset_action, sampled, targets, n_gx, tokens):
    frames = targets.shape[0]
    q, losses, mean = pl.pallas_call(
        functools.partial(critic_kernel, n_gx=n_gx, tokens=tokens),
        out_shape=(
            jax.ShapeDtypeStruct((frames, head_w.shape[1]), F32),
            jax.ShapeDtypeStruct((frames, 1), F32),
            jax.ShapeDtypeStruct((1, 1), F32),
        ),
        in_specs=[vmem()] * 6,
        out_specs=(vmem(),) * 3,
        compiler_params=pltpu.CompilerParams(vmem_limit_bytes=VMEM_LIMIT),
        name="critic",
    )(sums, head_w, head_b[None, :], dataset_action[:, None], sampled, targets[:, None])
    return q, losses.reshape(frames), mean.reshape(())


def shards(
    images, position, stem_w, stem_b, patch_w, norm_one, qkv_w, q_gain, k_gain, out_w, norm_two,
    mlp_in, mlp_out, norm_last, head_w, head_b, dataset_action, sampled, targets,
):
    n_gy, n_gx = lax.axis_size("gy"), lax.axis_size("gx")
    frames = images.shape[0]
    group = n_gy * n_gx // frames
    assert group * frames == n_gy * n_gx and n_gy % group == 0
    embedded = embed(borders(images), position, stem_w, stem_b, patch_w)
    seq = regroup(embedded, n_gx, group).reshape(-1, embedded.shape[-1])
    q, kv = project(seq, norm_one, qkv_w, q_gain, k_gain)
    partial = layer(seq, q, share(kv, group), out_w, norm_two, mlp_in, mlp_out, norm_last)
    sums = collect(partial, n_gx, n_gy * n_gx)
    return critic(
        sums, head_w, head_b, dataset_action, sampled, targets, n_gx, seq.shape[0] * group
    )


def solution(mesh):
    in_specs = (P(None, "gy", "gx"), P("gy", "gx", None)) + (P(),) * 17
    return jax.shard_map(
        shards, mesh=mesh, in_specs=in_specs, out_specs=(P(), P(), P()), check_vma=False
    )
```

```python
import functools

import jax
import jax.numpy as jnp
import numpy as np
from jax import lax
from jax.experimental import pallas as pl
from jax.experimental.pallas import tpu as pltpu
from jax.sharding import PartitionSpec as P

HEAD_DIM = 64
PATCH = 14
eps = 1e-06
penalty_weight = 1.0
F32 = jnp.float32
BF16 = jnp.bfloat16
MESH = pl.DeviceIdType.MESH
VMEM_LIMIT = 56 * 1024 * 1024


def vmem():
    return pl.BlockSpec(memory_space=pltpu.VMEM)


def gelu(x):
    u = x * (0.7978845608028654 + (0.7978845608028654 * 0.044715) * (x * x))
    half = 0.5 * x
    return half + half * jnp.tanh(u)


def layer_norm(values, gain):
    centre = values - jnp.mean(values, -1, keepdims=True)
    spread = jnp.mean(centre * centre, -1, keepdims=True)
    return centre * lax.rsqrt(spread + eps) * gain


def band(stem_w):
    channels = stem_w.shape[1]
    rows = np.arange(9 * (PATCH + 2))
    row_off, rest = rows // (3 * (PATCH + 2)), rows % (3 * (PATCH + 2))
    col_in, colour = rest // 3, rest % 3
    col_out = np.arange(PATCH * channels) // channels
    wide = jnp.tile(stem_w, (1, PATCH))
    picks = np.zeros((3, rows.size, 27), np.float32)
    for col_off in range(3):
        picks[col_off, rows, row_off * 9 + col_off * 3 + colour] = 1
    spread = jnp.dot(jnp.asarray(picks.reshape(-1, 27), BF16), wide, preferred_element_type=F32)
    spread = spread.reshape(3, rows.size, -1)
    total = 0.0
    for col_off in range(3):
        keep = col_in[:, None] == col_out[None, :] + col_off
        total = total + jnp.where(keep, spread[col_off], 0.0)
    return total.astype(BF16)


def frames_kernel(
    n_gy, n_gx, group, tall_ref, pos_ref, band_ref, bias_ref, pw_hbm, out_ref,
    ext, row_in, edge_out, edge_in, stem, pw, acc, made, load_sem, side_send, side_recv, send_sem,
    recv_sem,
):
    rows, frames, lanes = tall_ref.shape
    patch_rows, patch_cols, width = pos_ref.shape
    feats = band_ref.shape[1]
    reach = 3 * (PATCH + 2)
    parts = made.shape[0]
    part_cols = patch_cols // parts
    tiles = part_cols * patch_rows
    count = tiles * frames
    gy, gx = lax.axis_index("gy"), lax.axis_index("gx")
    low = lax.rem(gy, group)
    me = (gy // group) * n_gx + gx
    load = pltpu.make_async_copy(pw_hbm, pw, load_sem)
    load.start()

    def device(frame):
        return ((frame // n_gx) * group + low, lax.rem(frame, n_gx))

    above = (lax.rem(gy + n_gy - 1, n_gy), gx)
    below = (lax.rem(gy + 1, n_gy), gx)
    before = (gy, lax.rem(gx + n_gx - 1, n_gx))
    after = (gy, lax.rem(gx + 1, n_gx))
    barrier = pltpu.get_barrier_semaphore()
    for side in (above, below, before, after):
        pl.semaphore_signal(barrier, inc=1, device_id=side, device_id_type=MESH)

    def greet(k, carry):
        pl.semaphore_signal(
            barrier, inc=1, device_id=device(lax.rem(me + k, frames)), device_id_type=MESH
        )
        return carry

    lax.fori_loop(1, frames, greet, 0)
    pl.semaphore_wait(barrier, frames + 3)

    def side_copy(k, src, dst, side):
        return pltpu.make_async_remote_copy(
            src_ref=src, dst_ref=dst, send_sem=side_send.at[k], recv_sem=side_recv.at[k],
            device_id=side, device_id_type=MESH,
        )

    vertical = [
        side_copy(0, tall_ref.at[rows - 1], row_in.at[0], below),
        side_copy(1, tall_ref.at[0], row_in.at[1], above),
    ]
    for one in vertical:
        one.start()
    ext[1 : rows + 1] = tall_ref[...]
    for one in vertical:
        one.wait()
    ext[0] = jnp.where(gy > 0, row_in[0], jnp.zeros_like(row_in[0]))
    ext[rows + 1] = jnp.where(gy < n_gy - 1, row_in[1], jnp.zeros_like(row_in[1]))
    edge_out[0] = jnp.concatenate([ext[r, :, lanes - 3 :] for r in range(rows + 2)], axis=-1)
    edge_out[1] = jnp.concatenate([ext[r, :, :3] for r in range(rows + 2)], axis=-1)
    level = [
        side_copy(2, edge_out.at[0], edge_in.at[0], after),
        side_copy(3, edge_out.at[1], edge_in.at[1], before),
    ]
    for one in level:
        one.start()

    def edge(k, inside):
        got = edge_in[k]
        got = jnp.where(inside, got, jnp.zeros_like(got))
        return jnp.stack([got[:, 3 * r : 3 * r + 3] for r in range(rows + 2)], axis=0)

    order = list(range(1, patch_cols - 1)) + [0, patch_cols - 1]
    for part in range(parts):
        for spot in range(part_cols):
            col = order[part * part_cols + spot]
            if col == 0:
                for one in level:
                    one.wait()
                cut = jnp.concatenate([edge(0, gx > 0), ext[:, :, : reach - 3]], axis=-1)
            elif col == patch_cols - 1:
                cut = jnp.concatenate(
                    [ext[:, :, lanes - reach + 3 :], edge(1, gx < n_gx - 1)], axis=-1
                )
            else:
                at = 3 * PATCH * col - 3
                cut = ext[:, :, at : at + reach]
            taps = jnp.concatenate([cut[off : off + rows] for off in range(3)], axis=-1)
            for i in range(patch_rows):
                piece = taps[i * PATCH : (i + 1) * PATCH].reshape(PATCH * frames, 3 * reach)
                conv = jnp.dot(piece, band_ref[...], preferred_element_type=F32)
                stem[:, spot, i] = (
                    gelu(conv + bias_ref[...]).astype(BF16).reshape(PATCH, frames, feats)
                )
        if part == 0:
            load.wait()
        acc[...] = jnp.zeros_like(acc)

        def step(p, carry):
            acc[...] += jnp.dot(
                stem[p].reshape(count, feats),
                pw[pl.ds(pl.multiple_of(p * feats, 64), feats), :],
                preferred_element_type=F32,
            )
            return carry

        lax.fori_loop(0, PATCH, step, 0)
        pieces = []
        for spot in range(part_cols):
            col = order[part * part_cols + spot]
            for i in range(patch_rows):
                at = (spot * patch_rows + i) * frames
                place = pos_ref[i, col : col + 1, :].astype(F32)
                pieces.append((acc[at : at + frames, :] + place).astype(BF16))
        to = lax.broadcasted_iota(jnp.int32, (count, count), 0)
        fro = lax.broadcasted_iota(jnp.int32, (count, count), 1)
        swap = jnp.where((to % tiles) * frames + to // tiles == fro, 1.0, 0.0).astype(BF16)
        made[part] = (
            jnp.dot(swap, jnp.concatenate(pieces, axis=0), preferred_element_type=F32)
            .astype(BF16)
            .reshape(frames, tiles, width)
        )

        def start(k, carry):
            to = lax.rem(me + k, frames)
            pltpu.make_async_remote_copy(
                src_ref=made.at[part, to], dst_ref=out_ref.at[me, part],
                send_sem=send_sem.at[part, k], recv_sem=recv_sem.at[part, k],
                device_id=device(to), device_id_type=MESH,
            ).start()
            return carry

        lax.fori_loop(1, frames, start, 0)
        out_ref[me, part] = made[part, me]

    for part in range(parts):

        def finish(k, carry):
            fro = lax.rem(me - k + frames, frames)
            pltpu.make_async_remote_copy(
                src_ref=made.at[part, fro], dst_ref=out_ref.at[fro, part],
                send_sem=send_sem.at[part, k], recv_sem=recv_sem.at[part, k],
                device_id=device(fro), device_id_type=MESH,
            ).wait()
            return carry

        lax.fori_loop(1, frames, finish, 0)


def own_frames(images, position, stem_w, stem_b, patch_w, n_gy, n_gx, group):
    tall = jnp.transpose(images, (1, 0, 2))
    rows, frames, lanes = tall.shape
    patch_rows, patch_cols, width = position.shape
    feats = PATCH * stem_w.shape[1]
    parts = max(1, patch_rows * patch_cols // 16)
    tiles = patch_rows * patch_cols // parts
    edges = 3 * (rows + 2)
    return pl.pallas_call(
        functools.partial(frames_kernel, n_gy, n_gx, group),
        out_shape=jax.ShapeDtypeStruct((frames, parts, tiles, width), BF16),
        in_specs=[vmem()] * 4 + [pl.BlockSpec(memory_space=pl.ANY)],
        out_specs=vmem(),
        scratch_shapes=[
            pltpu.VMEM((rows + 2, frames, lanes), BF16),
            pltpu.VMEM((2, frames, lanes), BF16),
            pltpu.VMEM((2, frames, edges), BF16),
            pltpu.VMEM((2, frames, edges), BF16),
            pltpu.VMEM((PATCH, patch_cols // parts, patch_rows, frames, feats), BF16),
            pltpu.VMEM(patch_w.shape, BF16),
            pltpu.VMEM((tiles * frames, width), F32),
            pltpu.VMEM((parts, frames, tiles, width), BF16),
            pltpu.SemaphoreType.DMA,
            pltpu.SemaphoreType.DMA((4,)),
            pltpu.SemaphoreType.DMA((4,)),
            pltpu.SemaphoreType.DMA((parts, frames)),
            pltpu.SemaphoreType.DMA((parts, frames)),
        ],
        compiler_params=pltpu.CompilerParams(
            collective_id=0, has_side_effects=True, vmem_limit_bytes=VMEM_LIMIT
        ),
        name="own_frames",
    )(tall, position, band(stem_w), jnp.tile(stem_b, PATCH)[None, :], patch_w)


def head_scale(tile, gain):
    left = lax.broadcasted_iota(jnp.int32, tile.shape, 1) < HEAD_DIM
    square = tile * tile
    one = jnp.sum(jnp.where(left, square, 0.0), -1, keepdims=True)
    two = jnp.sum(jnp.where(left, 0.0, square), -1, keepdims=True)
    scale = lax.rsqrt(jnp.where(left, one, two) * (1.0 / HEAD_DIM) + eps)
    return tile * scale * gain


def critic_kernel(
    n_gx, group, devices, tokens, seq_ref, norm_ref, w_ref, qg_ref, kg_ref, norm2_ref, last_ref,
    b_ref, act_ref, samp_ref, targ_ref, ow_hbm, wi_hbm, wo_hbm, hw_hbm, out_ref, loss_ref, mean_ref,
    q_ref, kv_ref, attended, ow, wi, wo, hw, sums, load_sem, kv_send, kv_recv, send_sem, recv_sem,
):
    count, width = seq_ref.shape
    hidden = wi.shape[1]
    frames, actions = out_ref.shape
    pair = 2 * HEAD_DIM
    loads = [
        pltpu.make_async_copy(ow_hbm, ow, load_sem.at[0]),
        pltpu.make_async_copy(wi_hbm, wi, load_sem.at[1]),
        pltpu.make_async_copy(wo_hbm, wo, load_sem.at[2]),
        pltpu.make_async_copy(hw_hbm, hw, load_sem.at[3]),
    ]
    for load in loads:
        load.start()
    gy, gx = lax.axis_index("gy"), lax.axis_index("gx")
    low = lax.rem(gy, group)
    base = gy - low
    me = gy * n_gx + gx

    def device(other):
        return (other // n_gx, lax.rem(other, n_gx))

    barrier = pltpu.get_barrier_semaphore()

    def greet(k, carry):
        pl.semaphore_signal(
            barrier, inc=1, device_id=device(lax.rem(me + k, devices)), device_id_type=MESH
        )
        return carry

    lax.fori_loop(1, devices, greet, 0)

    def kv_copy(k, which, slot):
        return pltpu.make_async_remote_copy(
            src_ref=kv_ref.at[slot, which], dst_ref=kv_ref.at[slot, which],
            send_sem=kv_send.at[which, k], recv_sem=kv_recv.at[which, k],
            device_id=(base + lax.rem(low + k, group), gx), device_id_type=MESH,
        )

    def kv_start(which):
        def start(k, carry):
            kv_copy(k, which, low).start()
            return carry

        lax.fori_loop(1, group, start, 0)

    def kv_finish(which):
        def finish(k, carry):
            kv_copy(k, which, lax.rem(low - k + group, group)).wait()
            return carry

        lax.fori_loop(1, group, finish, 0)

    normed = layer_norm(seq_ref[...].astype(F32), norm_ref[...].reshape(1, width)).astype(BF16)
    q_gain = qg_ref[...].reshape(1, width)
    k_gain = kg_ref[...].reshape(1, width)

    def project(block):
        for at in range(0, width, 2 * pair):
            both = jnp.dot(
                normed,
                w_ref[:, block * width + at : block * width + at + 2 * pair],
                preferred_element_type=F32,
            )
            for half in range(2):
                tile = both[:, half * pair : (half + 1) * pair]
                lanes = slice(at + half * pair, at + half * pair + pair)
                if block == 0:
                    scaled = head_scale(tile, q_gain[:, lanes]) * HEAD_DIM ** (-0.5)
                    q_ref[:, lanes] = scaled.astype(BF16)
                elif block == 1:
                    kv_ref[low, 0, :, lanes] = head_scale(tile, k_gain[:, lanes]).astype(BF16)
                else:
                    kv_ref[low, 1, :, lanes] = tile.astype(BF16)

    project(2)
    pl.semaphore_wait(barrier, devices - 1)
    kv_start(1)
    project(1)
    kv_start(0)
    project(0)
    kv_finish(1)
    kv_finish(0)

    def attend(lanes, rows):
        q = q_ref[rows, lanes]
        left = lax.broadcasted_iota(jnp.int32, q.shape, 1) < HEAD_DIM
        halves = []
        for side in range(2):
            mine = jnp.where(left if side == 0 else jnp.logical_not(left), q, jnp.zeros_like(q))
            scores = [
                lax.dot_general(
                    mine, kv_ref[g, 0, :, lanes], (((1,), (1,)), ((), ())),
                    preferred_element_type=F32,
                )
                for g in range(group)
            ]
            top = functools.reduce(
                jnp.maximum, [jnp.max(part, -1, keepdims=True) for part in scores]
            )
            totals, mixed = 0.0, 0.0
            for g in range(group):
                expd = jnp.exp(scores[g] - top)
                totals = totals + jnp.sum(expd, -1, keepdims=True)
                mixed = mixed + jnp.dot(
                    expd.astype(BF16), kv_ref[g, 1, :, lanes], preferred_element_type=F32
                )
            halves.append(mixed / totals)
        attended[rows, lanes] = jnp.where(left, halves[0], halves[1]).astype(BF16)

    depth = max(32, 512 // group)

    def each(step, carry):
        at = pl.multiple_of((step // (count // depth)) * pair, pair)
        first = pl.multiple_of(lax.rem(step, count // depth) * depth, depth)
        attend(pl.ds(at, pair), pl.ds(first, depth))
        return carry

    lax.fori_loop(0, (width // pair) * (count // depth), each, 0)

    for load in loads:
        load.wait()
    block = 256
    total = jnp.zeros((1, width), F32)
    for first in range(0, count, block):
        rows = slice(first, first + block)
        stream = seq_ref[rows, :].astype(F32) + jnp.dot(
            attended[rows, :], ow[...], preferred_element_type=F32
        )
        normed2 = layer_norm(stream, norm2_ref[...].reshape(1, width)).astype(BF16)
        final = stream
        for at in range(0, hidden, width):
            inner = gelu(
                jnp.dot(normed2, wi[:, at : at + width], preferred_element_type=F32)
            ).astype(BF16)
            final = final + jnp.dot(inner, wo[at : at + width, :], preferred_element_type=F32)
        total = total + jnp.sum(
            layer_norm(final, last_ref[...].reshape(1, width)), 0, keepdims=True
        )
    sums[me] = total

    def sum_copy(k, slot):
        return pltpu.make_async_remote_copy(
            src_ref=sums.at[slot], dst_ref=sums.at[slot],
            send_sem=send_sem.at[k], recv_sem=recv_sem.at[k],
            device_id=device(lax.rem(me + k, devices)), device_id_type=MESH,
        )

    def start(k, carry):
        sum_copy(k, me).start()
        return carry

    def finish(k, carry):
        sum_copy(k, lax.rem(me - k + devices, devices)).wait()
        return carry

    lax.fori_loop(1, devices, start, 0)
    lax.fori_loop(1, devices, finish, 0)

    pieces = []
    for frame in range(frames):
        part = 0.0
        for other in range(group):
            part = part + sums[((frame // n_gx) * group + other) * n_gx + frame % n_gx]
        pieces.append(part)
    rest = jnp.concatenate(pieces, axis=0) / tokens
    q = 0.0
    for _ in range(3):
        piece = rest.astype(BF16)
        rest = rest - piece.astype(F32)
        q = q + jnp.dot(piece, hw[...], preferred_element_type=F32)
    q = q + b_ref[...].reshape(1, actions)
    out_ref[...] = q
    columns = lax.broadcasted_iota(jnp.int32, (frames, actions), 1)
    same = lax.broadcasted_iota(jnp.int32, (frames, frames), 0) == lax.broadcasted_iota(
        jnp.int32, (frames, frames), 1
    )

    def upright(row):
        return jnp.sum(jnp.where(same, row.astype(F32).reshape(1, frames), 0.0), -1, keepdims=True)

    def pick(index):
        return jnp.sum(jnp.where(index == columns, q, 0.0), -1, keepdims=True)

    chosen = pick(upright(act_ref[...]).astype(jnp.int32))
    picked = [pick(samp_ref[:, s : s + 1]) for s in range(samp_ref.shape[1])]
    top = functools.reduce(jnp.maximum, picked)
    spread = top + jnp.log(sum(jnp.exp(one - top) for one in picked))
    loss = penalty_weight * (spread - chosen) + 0.5 * (chosen - upright(targ_ref[...])) ** 2
    loss_ref[...] = jnp.sum(jnp.where(same, loss, 0.0), 0, keepdims=True)
    mean_ref[...] = jnp.mean(loss, 0, keepdims=True)


def critic(
    seq, norm_one, qkv_w, q_gain, k_gain, norm_two, norm_last, head_b, dataset_action, sampled,
    targets, out_w, mlp_in, mlp_out, head_w, n_gx, group, devices,
):
    count, width = seq.shape
    frames = targets.shape[0]
    q, losses, mean = pl.pallas_call(
        functools.partial(critic_kernel, n_gx, group, devices, count * group),
        out_shape=(
            jax.ShapeDtypeStruct((frames, head_w.shape[1]), F32),
            jax.ShapeDtypeStruct((1, frames), F32),
            jax.ShapeDtypeStruct((1, 1), F32),
        ),
        in_specs=[vmem()] * 11 + [pl.BlockSpec(memory_space=pl.ANY)] * 4,
        out_specs=(vmem(),) * 3,
        scratch_shapes=[
            pltpu.VMEM((count, width), BF16),
            pltpu.VMEM((group, 2, count, width), BF16),
            pltpu.VMEM((count, width), BF16),
            pltpu.VMEM(out_w.shape, BF16),
            pltpu.VMEM(mlp_in.shape, BF16),
            pltpu.VMEM(mlp_out.shape, BF16),
            pltpu.VMEM(head_w.shape, BF16),
            pltpu.VMEM((devices, 1, width), F32),
            pltpu.SemaphoreType.DMA((4,)),
            pltpu.SemaphoreType.DMA((2, group)),
            pltpu.SemaphoreType.DMA((2, group)),
            pltpu.SemaphoreType.DMA((devices,)),
            pltpu.SemaphoreType.DMA((devices,)),
        ],
        compiler_params=pltpu.CompilerParams(
            collective_id=1, has_side_effects=True, vmem_limit_bytes=VMEM_LIMIT
        ),
        name="critic",
    )(
        seq, norm_one, qkv_w, q_gain, k_gain, norm_two, norm_last, head_b, dataset_action, sampled,
        targets, out_w, mlp_in, mlp_out, head_w,
    )
    return q, losses.reshape(frames), mean.reshape(())


def shards(
    images, position, stem_w, stem_b, patch_w, norm_one, qkv_w, q_gain, k_gain, out_w, norm_two,
    mlp_in, mlp_out, norm_last, head_w, head_b, dataset_action, sampled, targets,
):
    n_gy, n_gx = lax.axis_size("gy"), lax.axis_size("gx")
    group = n_gy * n_gx // images.shape[0]
    assert group * images.shape[0] == n_gy * n_gx and n_gy % group == 0
    embedded = own_frames(images, position, stem_w, stem_b, patch_w, n_gy, n_gx, group)
    return critic(
        embedded.reshape(-1, embedded.shape[-1]), norm_one, qkv_w, q_gain, k_gain, norm_two,
        norm_last, head_b, dataset_action, sampled, targets, out_w, mlp_in, mlp_out, head_w,
        n_gx, group, n_gy * n_gx,
    )


def solution(mesh):
    in_specs = (P(None, "gy", "gx"), P("gy", "gx", None)) + (P(),) * 17
    return jax.shard_map(
        shards, mesh=mesh, in_specs=in_specs, out_specs=(P(), P(), P()), check_vma=False
    )
```

```python
import functools

import jax
import jax.numpy as jnp
from jax import lax
from jax.experimental import pallas as pl
from jax.experimental.pallas import tpu as pltpu
from jax.sharding import PartitionSpec as P

HEAD_DIM = 64
PATCH = 14
eps = 1e-06
penalty_weight = 1.0
F32 = jnp.float32
BF16 = jnp.bfloat16
MESH = pl.DeviceIdType.MESH
VMEM_LIMIT = 60 * 1024 * 1024


def vmem():
    return pl.BlockSpec(memory_space=pltpu.VMEM)


def gelu(x):
    u = x * (0.7978845608028654 + (0.7978845608028654 * 0.044715) * (x * x))
    half = 0.5 * x
    return half + half * jnp.tanh(u)


def layer_norm(values, gain):
    centre = values - jnp.mean(values, -1, keepdims=True)
    spread = jnp.mean(centre * centre, -1, keepdims=True)
    return centre * lax.rsqrt(spread + eps) * gain


def band(stem_w, length):
    wide = jnp.concatenate([stem_w] * length, axis=-1)
    channels = stem_w.shape[1]
    reach = 3 * (length + 2)

    def grid(shape):
        return [lax.broadcasted_iota(jnp.int32, shape, axis) for axis in range(2)]

    row, tap = grid((3 * reach, 27))
    place, lane = grid((3 * reach, length * channels))
    total = 0.0
    for off in range(3):
        picks = tap == (row // reach) * 9 + off * 3 + row % 3
        spread = jnp.dot(
            jnp.where(picks, 1.0, 0.0).astype(BF16), wide, preferred_element_type=F32
        )
        total = total + jnp.where((place % reach) // 3 == lane // channels + off, spread, 0.0)
    return total.astype(BF16)


def head_scale(tile, gain):
    left = lax.broadcasted_iota(jnp.int32, tile.shape, 1) < HEAD_DIM
    square = tile * tile
    one = jnp.sum(jnp.where(left, square, 0.0), -1, keepdims=True)
    two = jnp.sum(jnp.where(left, 0.0, square), -1, keepdims=True)
    scale = lax.rsqrt(jnp.where(left, one, two) * (1.0 / HEAD_DIM) + eps)
    return tile * scale * gain


def whole_kernel(
    n_gy, n_gx, group, tall_ref, pos_ref, sw_ref, sb_ref, norm_ref, qg_ref, kg_ref, norm2_ref,
    last_ref, b_ref, act_ref, samp_ref, targ_ref, pw_hbm, qkv_hbm, ow_hbm, wi_hbm, wo_hbm, hw_hbm,
    out_ref, loss_ref, mean_ref, ext, row_in, edge_out, edge_in, band_ref, stem, pw, acc, made, got,
    q_ref, kv_ref, attended, w_ref, ow, wi, wo, hw, sums, load_sem, side_send, side_recv, send_sem,
    recv_sem, kv_send, kv_recv, sum_send, sum_recv,
):
    rows, frames, lanes = tall_ref.shape
    patch_rows, patch_cols, width = pos_ref.shape
    feats = band_ref.shape[1]
    pair = 2 * HEAD_DIM
    hidden = wi.shape[1]
    actions = out_ref.shape[1]
    devices = n_gy * n_gx
    reach = 3 * (PATCH + 2)
    parts = made.shape[0]
    part_cols = patch_cols // parts
    tiles = part_cols * patch_rows
    part_count = tiles * frames
    gy, gx = lax.axis_index("gy"), lax.axis_index("gx")
    low = lax.rem(gy, group)
    slot = (gy // group) * n_gx + gx
    pw_load = pltpu.make_async_copy(pw_hbm, pw, load_sem.at[0])
    pw_load.start()

    def owner(frame):
        return ((frame // n_gx) * group + low, lax.rem(frame, n_gx))

    above = (lax.rem(gy + n_gy - 1, n_gy), gx)
    below = (lax.rem(gy + 1, n_gy), gx)
    before = (gy, lax.rem(gx + n_gx - 1, n_gx))
    after = (gy, lax.rem(gx + 1, n_gx))
    me = gy * n_gx + gx
    base = gy - low

    def device(other):
        return (other // n_gx, lax.rem(other, n_gx))

    barrier = pltpu.get_barrier_semaphore()

    def greet(k, carry):
        pl.semaphore_signal(
            barrier, inc=1, device_id=device(lax.rem(me + k, devices)), device_id_type=MESH
        )
        return carry

    lax.fori_loop(1, devices, greet, 0)
    band_ref[...] = band(sw_ref[...], PATCH)
    bias = jnp.concatenate([sb_ref[...].reshape(1, -1)] * PATCH, axis=-1)
    pl.semaphore_wait(barrier, devices - 1)

    def side_copy(k, src, dst, side):
        return pltpu.make_async_remote_copy(
            src_ref=src, dst_ref=dst, send_sem=side_send.at[k], recv_sem=side_recv.at[k],
            device_id=side, device_id_type=MESH,
        )

    vertical = [
        side_copy(0, tall_ref.at[rows - 1], row_in.at[0], below),
        side_copy(1, tall_ref.at[0], row_in.at[1], above),
    ]
    for one in vertical:
        one.start()
    ext[1 : rows + 1] = tall_ref[...]
    for one in vertical:
        one.wait()
    ext[0] = jnp.where(gy > 0, row_in[0], jnp.zeros_like(row_in[0]))
    ext[rows + 1] = jnp.where(gy < n_gy - 1, row_in[1], jnp.zeros_like(row_in[1]))
    edge_out[0] = jnp.concatenate([ext[r, :, lanes - 3 :] for r in range(rows + 2)], axis=-1)
    edge_out[1] = jnp.concatenate([ext[r, :, :3] for r in range(rows + 2)], axis=-1)
    level = [
        side_copy(2, edge_out.at[0], edge_in.at[0], after),
        side_copy(3, edge_out.at[1], edge_in.at[1], before),
    ]
    for one in level:
        one.start()
    loads = [
        pltpu.make_async_copy(src, dst, load_sem.at[k + 1])
        for k, (src, dst) in enumerate(
            ((qkv_hbm, w_ref), (ow_hbm, ow), (wi_hbm, wi), (wo_hbm, wo), (hw_hbm, hw))
        )
    ]

    def edge(k, inside):
        got = edge_in[k]
        got = jnp.where(inside, got, jnp.zeros_like(got))
        return jnp.stack([got[:, 3 * r : 3 * r + 3] for r in range(rows + 2)], axis=0)

    order = list(range(1, patch_cols - 1)) + [0, patch_cols - 1]
    for part in range(parts):
        for spot in range(part_cols):
            col = order[part * part_cols + spot]
            if col == 0:
                for one in level:
                    one.wait()
                cut = jnp.concatenate([edge(0, gx > 0), ext[:, :, : reach - 3]], axis=-1)
            elif col == patch_cols - 1:
                cut = jnp.concatenate(
                    [ext[:, :, lanes - reach + 3 :], edge(1, gx < n_gx - 1)], axis=-1
                )
            else:
                at = 3 * PATCH * col - 3
                cut = ext[:, :, at : at + reach]
            taps = jnp.concatenate([cut[off : off + rows] for off in range(3)], axis=-1)
            for i in range(patch_rows):
                piece = taps[i * PATCH : (i + 1) * PATCH].reshape(PATCH * frames, 3 * reach)
                conv = jnp.dot(piece, band_ref[...], preferred_element_type=F32)
                stem[:, spot, i] = (
                    gelu(conv + bias).astype(BF16).reshape(PATCH, frames, feats)
                )
        if part == 0:
            pw_load.wait()
            for load in loads:
                load.start()
        acc[...] = jnp.zeros_like(acc)

        def step(p, carry):
            acc[...] += jnp.dot(
                stem[p].reshape(part_count, feats),
                pw[pl.ds(pl.multiple_of(p * feats, 64), feats), :],
                preferred_element_type=F32,
            )
            return carry

        lax.fori_loop(0, PATCH, step, 0)
        pieces = []
        for spot in range(part_cols):
            col = order[part * part_cols + spot]
            for i in range(patch_rows):
                at = (spot * patch_rows + i) * frames
                place = pos_ref[i, col : col + 1, :].astype(F32)
                pieces.append((acc[at : at + frames, :] + place).astype(BF16))
        to = lax.broadcasted_iota(jnp.int32, (part_count, part_count), 0)
        fro = lax.broadcasted_iota(jnp.int32, (part_count, part_count), 1)
        swap = jnp.where((to % tiles) * frames + to // tiles == fro, 1.0, 0.0).astype(BF16)
        made[part] = (
            jnp.dot(swap, jnp.concatenate(pieces, axis=0), preferred_element_type=F32)
            .astype(BF16)
            .reshape(frames, tiles, width)
        )

        def start(k, carry):
            to = lax.rem(slot + k, frames)
            pltpu.make_async_remote_copy(
                src_ref=made.at[part, to], dst_ref=got.at[slot, part],
                send_sem=send_sem.at[part, k], recv_sem=recv_sem.at[part, k],
                device_id=owner(to), device_id_type=MESH,
            ).start()
            return carry

        lax.fori_loop(1, frames, start, 0)
        got[slot, part] = made[part, slot]

    count = parts * part_count

    def sequence(part):
        return got[:, part].reshape(part_count, width)

    def kv_copy(k, which, part, place):
        rows = pl.ds(part * part_count, part_count)
        return pltpu.make_async_remote_copy(
            src_ref=kv_ref.at[place, which, rows], dst_ref=kv_ref.at[place, which, rows],
            send_sem=kv_send.at[which, part, k], recv_sem=kv_recv.at[which, part, k],
            device_id=(base + lax.rem(low + k, group), gx), device_id_type=MESH,
        )

    def kv_start(which, part):
        def start(k, carry):
            kv_copy(k, which, part, low).start()
            return carry

        lax.fori_loop(1, group, start, 0)

    def kv_finish(which, part):
        def finish(k, carry):
            kv_copy(k, which, part, lax.rem(low - k + group, group)).wait()
            return carry

        lax.fori_loop(1, group, finish, 0)

    q_gain = qg_ref[...].reshape(1, width)
    k_gain = kg_ref[...].reshape(1, width)

    def project(normed, block, part):
        rows = slice(part * part_count, (part + 1) * part_count)
        for at in range(0, width, 2 * pair):
            both = jnp.dot(
                normed,
                w_ref[:, block * width + at : block * width + at + 2 * pair],
                preferred_element_type=F32,
            )
            for half in range(2):
                tile = both[:, half * pair : (half + 1) * pair]
                lanes = slice(at + half * pair, at + half * pair + pair)
                if block == 0:
                    scaled = head_scale(tile, q_gain[:, lanes]) * HEAD_DIM ** (-0.5)
                    q_ref[rows, lanes] = scaled.astype(BF16)
                elif block == 1:
                    kv_ref[low, 0, rows, lanes] = head_scale(tile, k_gain[:, lanes]).astype(BF16)
                else:
                    kv_ref[low, 1, rows, lanes] = tile.astype(BF16)

    loads[0].wait()
    for part in range(parts):

        def finish(k, carry):
            fro = lax.rem(slot - k + frames, frames)
            pltpu.make_async_remote_copy(
                src_ref=made.at[part, fro], dst_ref=got.at[fro, part],
                send_sem=send_sem.at[part, k], recv_sem=recv_sem.at[part, k],
                device_id=owner(fro), device_id_type=MESH,
            ).wait()
            return carry

        lax.fori_loop(1, frames, finish, 0)
        normed = layer_norm(
            sequence(part).astype(F32), norm_ref[...].reshape(1, width)
        ).astype(BF16)
        project(normed, 2, part)
        kv_start(1, part)
        project(normed, 1, part)
        kv_start(0, part)
        project(normed, 0, part)
    for part in range(parts):
        kv_finish(1, part)
        kv_finish(0, part)

    def attend(lanes, rows):
        q = q_ref[rows, lanes]
        left = lax.broadcasted_iota(jnp.int32, q.shape, 1) < HEAD_DIM
        halves = []
        for side in range(2):
            mine = jnp.where(left if side == 0 else jnp.logical_not(left), q, jnp.zeros_like(q))
            scores = [
                lax.dot_general(
                    mine, kv_ref[g, 0, :, lanes], (((1,), (1,)), ((), ())),
                    preferred_element_type=F32,
                )
                for g in range(group)
            ]
            top = functools.reduce(
                jnp.maximum, [jnp.max(part, -1, keepdims=True) for part in scores]
            )
            totals, mixed = 0.0, 0.0
            for g in range(group):
                expd = jnp.exp(scores[g] - top)
                totals = totals + jnp.sum(expd, -1, keepdims=True)
                mixed = mixed + jnp.dot(
                    expd.astype(BF16), kv_ref[g, 1, :, lanes], preferred_element_type=F32
                )
            halves.append(mixed / totals)
        attended[rows, lanes] = jnp.where(left, halves[0], halves[1]).astype(BF16)

    depth = max(32, 512 // group)

    def each(step, carry):
        at = pl.multiple_of((step // (count // depth)) * pair, pair)
        first = pl.multiple_of(lax.rem(step, count // depth) * depth, depth)
        attend(pl.ds(at, pair), pl.ds(first, depth))
        return carry

    lax.fori_loop(0, (width // pair) * (count // depth), each, 0)

    for load in loads[1:]:
        load.wait()
    total = jnp.zeros((1, width), F32)
    for part in range(parts):
        rows = slice(part * part_count, (part + 1) * part_count)
        stream = sequence(part).astype(F32) + jnp.dot(
            attended[rows, :], ow[...], preferred_element_type=F32
        )
        normed2 = layer_norm(stream, norm2_ref[...].reshape(1, width)).astype(BF16)
        final = stream
        for at in range(0, hidden, width):
            inner = gelu(
                jnp.dot(normed2, wi[:, at : at + width], preferred_element_type=F32)
            ).astype(BF16)
            final = final + jnp.dot(inner, wo[at : at + width, :], preferred_element_type=F32)
        total = total + jnp.sum(
            layer_norm(final, last_ref[...].reshape(1, width)), 0, keepdims=True
        )
    sums[me] = total

    def sum_copy(k, slot):
        return pltpu.make_async_remote_copy(
            src_ref=sums.at[slot], dst_ref=sums.at[slot],
            send_sem=sum_send.at[k], recv_sem=sum_recv.at[k],
            device_id=device(lax.rem(me + k, devices)), device_id_type=MESH,
        )

    def start(k, carry):
        sum_copy(k, me).start()
        return carry

    def finish(k, carry):
        sum_copy(k, lax.rem(me - k + devices, devices)).wait()
        return carry

    lax.fori_loop(1, devices, start, 0)
    lax.fori_loop(1, devices, finish, 0)

    pieces = []
    for frame in range(frames):
        added = 0.0
        for other in range(group):
            added = added + sums[((frame // n_gx) * group + other) * n_gx + frame % n_gx]
        pieces.append(added)
    rest = jnp.concatenate(pieces, axis=0) / (count * group)
    q = 0.0
    for _ in range(3):
        piece = rest.astype(BF16)
        rest = rest - piece.astype(F32)
        q = q + jnp.dot(piece, hw[...], preferred_element_type=F32)
    q = q + b_ref[...].reshape(1, actions)
    out_ref[...] = q
    columns = lax.broadcasted_iota(jnp.int32, (frames, actions), 1)
    same = lax.broadcasted_iota(jnp.int32, (frames, frames), 0) == lax.broadcasted_iota(
        jnp.int32, (frames, frames), 1
    )

    def upright(row):
        return jnp.sum(jnp.where(same, row.astype(F32).reshape(1, frames), 0.0), -1, keepdims=True)

    def pick(index):
        return jnp.sum(jnp.where(index == columns, q, 0.0), -1, keepdims=True)

    chosen = pick(upright(act_ref[...]).astype(jnp.int32))
    picked = [pick(samp_ref[:, s : s + 1]) for s in range(samp_ref.shape[1])]
    top = functools.reduce(jnp.maximum, picked)
    spread = top + jnp.log(sum(jnp.exp(one - top) for one in picked))
    loss = penalty_weight * (spread - chosen) + 0.5 * (chosen - upright(targ_ref[...])) ** 2
    loss_ref[...] = jnp.sum(jnp.where(same, loss, 0.0), 0, keepdims=True)
    mean_ref[...] = jnp.mean(loss, 0, keepdims=True)


def shards(
    images, position, stem_w, stem_b, patch_w, norm_one, qkv_w, q_gain, k_gain, out_w, norm_two,
    mlp_in, mlp_out, norm_last, head_w, head_b, dataset_action, sampled, targets,
):
    n_gy, n_gx = lax.axis_size("gy"), lax.axis_size("gx")
    devices = n_gy * n_gx
    group = devices // images.shape[0]
    assert group * images.shape[0] == devices and n_gy % group == 0
    tall = jnp.transpose(images, (1, 0, 2))
    rows, frames, lanes = tall.shape
    patch_rows, patch_cols, width = position.shape
    feats = PATCH * stem_w.shape[1]
    parts = max(1, patch_rows * patch_cols // 16)
    tiles = patch_rows * patch_cols // parts
    edges = 3 * (rows + 2)
    count = frames * tiles * parts
    dma = pltpu.SemaphoreType.DMA
    q, losses, mean = pl.pallas_call(
        functools.partial(whole_kernel, n_gy, n_gx, group),
        out_shape=(
            jax.ShapeDtypeStruct((frames, head_w.shape[1]), F32),
            jax.ShapeDtypeStruct((1, frames), F32),
            jax.ShapeDtypeStruct((1, 1), F32),
        ),
        in_specs=[vmem()] * 13 + [pl.BlockSpec(memory_space=pl.ANY)] * 6,
        out_specs=(vmem(),) * 3,
        scratch_shapes=[
            pltpu.VMEM((rows + 2, frames, lanes), BF16),
            pltpu.VMEM((2, frames, lanes), BF16),
            pltpu.VMEM((2, frames, edges), BF16),
            pltpu.VMEM((2, frames, edges), BF16),
            pltpu.VMEM((9 * (PATCH + 2), feats), BF16),
            pltpu.VMEM((PATCH, patch_cols // parts, patch_rows, frames, feats), BF16),
            pltpu.VMEM(patch_w.shape, BF16),
            pltpu.VMEM((tiles * frames, width), F32),
            pltpu.VMEM((parts, frames, tiles, width), BF16),
            pltpu.VMEM((frames, parts, tiles, width), BF16),
            pltpu.VMEM((count, width), BF16),
            pltpu.VMEM((group, 2, count, width), BF16),
            pltpu.VMEM((count, width), BF16),
            pltpu.VMEM(qkv_w.shape, BF16),
            pltpu.VMEM(out_w.shape, BF16),
            pltpu.VMEM(mlp_in.shape, BF16),
            pltpu.VMEM(mlp_out.shape, BF16),
            pltpu.VMEM(head_w.shape, BF16),
            pltpu.VMEM((devices, 1, width), F32),
            dma((6,)),
            dma((4,)),
            dma((4,)),
            dma((parts, frames)),
            dma((parts, frames)),
            dma((2, parts, group)),
            dma((2, parts, group)),
            dma((devices,)),
            dma((devices,)),
        ],
        compiler_params=pltpu.CompilerParams(
            collective_id=0, has_side_effects=True, vmem_limit_bytes=VMEM_LIMIT
        ),
        name="whole",
    )(
        tall, position, stem_w, stem_b, norm_one, q_gain, k_gain, norm_two, norm_last, head_b,
        dataset_action, sampled, targets, patch_w, qkv_w, out_w, mlp_in, mlp_out, head_w,
    )
    return q, losses.reshape(frames), mean.reshape(())


def solution(mesh):
    in_specs = (P(None, "gy", "gx"), P("gy", "gx", None)) + (P(),) * 17
    return jax.shard_map(
        shards, mesh=mesh, in_specs=in_specs, out_specs=(P(), P(), P()), check_vma=False
    )
```
